32 devices in a mesh: snp: 2 (over y), samp: 16 (over z, x, core).
Axes of the slice: x: 2, y: 2, z: 4, core: 2. Of those that a mesh axis runs over, the one named last changes fastest.
Arguments:
- dosages: bfloat16 [12288, 1024], P('samp', 'snp'), may hold values from 0 to 2
- residual: float32 [12288], P('samp'), may hold values from -40 to 40
- pair_list: int32 [4, 2], replicated, may hold values from 0 to 3, as said below
- block_slot: int32 [4], replicated, may hold values from 0 to 3, as said below
- pair_counts: int32 [4], replicated, may hold values from 3072 to 12288, as said below
Outputs:
- epistasis_score: float32 [1024], P('snp')
The draws below stay inside these ranges and needn't reach their ends.
Inputs may be any that keep to these rules, and one draw needn't show every extreme that they name: `pair_list`: block b is paired with block (b + 1) mod 4, each such pair listed once, in some order and orientation. Counting each pair at the snp group block_slot[first block] // 2, no group gets more than 4 pairs and one group gets exactly 4. A permutation: block b is stored in columns block_slot[b] * 256 onward, on snp group block_slot[b] // 2. Pair p uses the samples with index below pair_counts[p]; some pair uses all 12288.
All inputs are finite; a program needn't handle non-finite values.
Results may differ from the reference program's by a relative error of at most 0.0021.
Values may be sent and summed in bfloat16 or wider, within the bound.
A program may use at most 64 MiB of HBM per device.

```python
import math
import jax
import jax.numpy as jnp
from jax import lax

BLOCK = 256
NBLK = 4
SNPS = 1024
SAMPLES = 12288
PAIRS = 4


def pair_tables(key):
    base = jax.random.fold_in(key, 7)
    key_perm, key_order = jax.random.split(base, 2)
    block_ids = jnp.arange(NBLK, dtype=jnp.int32)
    slot_of_block = jax.random.permutation(key_perm, NBLK).astype(jnp.int32)
    block_of_slot = jnp.argsort(slot_of_block).astype(jnp.int32)
    partner_slot = jnp.bitwise_xor(slot_of_block[0], 1)
    partner = block_of_slot[partner_slot]
    clash = jnp.logical_or(partner == 1, partner == NBLK - 1)
    slot_partner = slot_of_block[partner]
    slot_two = slot_of_block[2]
    moved = jnp.where(block_ids == partner, slot_two, jnp.where(block_ids == 2, slot_partner, slot_of_block))
    slot_of_block = jnp.where(clash, moved, slot_of_block).astype(jnp.int32)
    hot_group = slot_of_block[0] // 2
    first = block_ids
    second = jnp.remainder(block_ids + 1, NBLK).astype(jnp.int32)
    slot_a = slot_of_block[first]
    slot_b = slot_of_block[second]
    hot_a = slot_a // 2 == hot_group
    hot_b = slot_b // 2 == hot_group
    turn = jnp.logical_or(jnp.logical_and(hot_b, jnp.logical_not(hot_a)), jnp.logical_and(jnp.logical_not(jnp.logical_or(hot_a, hot_b)), slot_b > slot_a))
    block_a = jnp.where(turn, second, first)
    block_b = jnp.where(turn, first, second)
    order = jax.random.permutation(key_order, PAIRS)
    listed = jnp.stack([block_a[order], block_b[order]], axis=1)
    return (listed.astype(jnp.int32), slot_of_block)


def draw_pair_list(key, part):
    return pair_tables(key)[0]


def draw_block_slot(key, part):
    return pair_tables(key)[1]


def draw_pair_counts(key, part):
    counts = jax.random.randint(jax.random.fold_in(key, 11), (PAIRS,), SAMPLES // 4, SAMPLES + 1)
    return counts.at[0].set(SAMPLES).astype(jnp.int32)


def draw_residual(key, part):
    base_key = jax.random.fold_in(key, 13)
    key_base, key_scale = jax.random.split(base_key)
    place = jnp.arange(SAMPLES, dtype=jnp.float32) / SAMPLES
    spread = jnp.exp(jax.random.uniform(key_scale, (SAMPLES,), jnp.float32, 0.0, math.log(10.0)))
    values = jnp.clip(jax.random.normal(key_base, (SAMPLES,), jnp.float32), -4.0, 4.0)
    rising = 1.0 + 2.0 * place
    return values * spread * rising * 0.25


def draw_dosages(key, part):
    base_key = jax.random.fold_in(key, 17)
    key_unit, key_rare, key_load, key_anc = jax.random.split(base_key, 4)
    rare_low = 2.0
    rare_high = 200.0
    strength = 0.4
    rareness = jnp.exp(jax.random.uniform(key_rare, (SNPS,), jnp.float32, math.log(rare_low), math.log(rare_high)))
    loading = jax.random.uniform(key_load, (2, SNPS), jnp.float32, -1.0, 1.0)
    ancestry = jax.random.uniform(key_anc, (SAMPLES, 2), jnp.float32, -1.0, 1.0)
    shift = ancestry[:, 0:1] * loading[0][None, :] + ancestry[:, 1:2] * loading[1][None, :]
    exponent = rareness[None, :] * jnp.exp(strength * shift)
    unit = jax.random.uniform(key_unit, (SAMPLES, SNPS), jnp.float32, 1e-06, 1.0)
    return (2.0 * jnp.exp(jnp.maximum(exponent * jnp.log(unit), -36.0))).astype(jnp.bfloat16)


def setup_inputs(seed: int = 0) -> dict:
    key_of = jax.random.split(jax.random.key(seed), 6)
    dosages = draw_dosages(jax.random.fold_in(key_of[5], 71), 0)
    residual = draw_residual(jax.random.fold_in(key_of[5], 71), 0)
    pair_list = draw_pair_list(jax.random.fold_in(key_of[5], 71), 0)
    block_slot = draw_block_slot(jax.random.fold_in(key_of[5], 71), 0)
    pair_counts = draw_pair_counts(jax.random.fold_in(key_of[5], 71), 0)
    return {"dosages": dosages, "residual": residual, "pair_list": pair_list, "block_slot": block_slot, "pair_counts": pair_counts}


def reference(dosages, residual, pair_list, block_slot, pair_counts):
    spread_var = jnp.sum(residual * residual) / SAMPLES
    position = jnp.arange(SAMPLES, dtype=jnp.int32)
    highest = lax.Precision.HIGHEST

    def one_pair(index, score):
        first_block = pair_list[index, 0]
        second_block = pair_list[index, 1]
        first_col = (block_slot[first_block] * BLOCK).astype(jnp.int32)
        second_col = (block_slot[second_block] * BLOCK).astype(jnp.int32)
        left = lax.dynamic_slice_in_dim(dosages, first_col, BLOCK, 1)
        right = lax.dynamic_slice_in_dim(dosages, second_col, BLOCK, 1)
        left_sq = left * left
        right_sq = right * right
        live = (position < pair_counts[index]).astype(jnp.float32)
        weighted = (left.astype(jnp.float32) * (residual * live)[:, None]).astype(jnp.bfloat16)
        masked = (right_sq.astype(jnp.float32) * live[:, None]).astype(jnp.bfloat16)
        cross = jnp.dot(weighted.astype(jnp.float32).T, right.astype(jnp.float32), precision=highest)
        moment = jnp.dot(left_sq.astype(jnp.float32).T, masked.astype(jnp.float32), precision=highest)
        zvalue = cross / jnp.sqrt(spread_var * moment + 1e-06)
        current = lax.dynamic_slice_in_dim(score, first_col, BLOCK, 0)
        score = lax.dynamic_update_slice_in_dim(score, current + lax.optimization_barrier(jnp.sum(zvalue, axis=1)), first_col, 0)
        current = lax.dynamic_slice_in_dim(score, second_col, BLOCK, 0)
        score = lax.dynamic_update_slice_in_dim(score, current + lax.optimization_barrier(jnp.sum(zvalue, axis=0)), second_col, 0)
        return score
    score = lax.fori_loop(0, PAIRS, one_pair, jnp.zeros((SNPS,), jnp.float32))
    return score / jnp.sqrt(jnp.float32(2 * BLOCK))
```

```python
import math

import jax
import jax.numpy as jnp
from jax import lax
from jax.experimental import pallas as pl
from jax.experimental.pallas import tpu as pltpu
from jax.sharding import PartitionSpec as P

BLOCK = 256


def any_groups(dosages, residual, pair_list, block_slot, pair_counts):
    local_rows = dosages.shape[0]
    groups = lax.axis_size("snp")
    shards = lax.axis_size("samp")
    total_rows = local_rows * shards
    blocks = block_slot.shape[0]
    num_pairs = pair_list.shape[0]
    highest = lax.Precision.HIGHEST
    gathered = lax.all_gather(dosages, "snp", axis=1, tiled=True)
    spread_sum = lax.psum(jnp.sum(residual * residual), "samp")
    spread_var = spread_sum / total_rows
    position = lax.axis_index("samp") * local_rows + jnp.arange(local_rows, dtype=jnp.int32)
    block_ids = jnp.arange(blocks, dtype=jnp.int32)
    slot_first = jnp.sum(
        (pair_list[:, 0:1] == block_ids[None, :]).astype(jnp.int32) * block_slot[None, :], axis=1
    )
    slot_second = jnp.sum(
        (pair_list[:, 1:2] == block_ids[None, :]).astype(jnp.int32) * block_slot[None, :], axis=1
    )
    group_id = lax.axis_index("snp")
    pair_ids = jnp.arange(num_pairs, dtype=jnp.int32)
    width_slots = (num_pairs + groups - 1) // groups
    wanted = group_id * width_slots + jnp.arange(width_slots, dtype=jnp.int32)
    picked = (pair_ids[:, None] == wanted[None, :]).astype(jnp.int32)
    live_slot = jnp.sum(picked, axis=0)
    first_at = jnp.sum(picked * slot_first[:, None], axis=0)
    second_at = jnp.sum(picked * slot_second[:, None], axis=0)
    count_at = jnp.sum(picked * pair_counts[:, None], axis=0)
    live_rows = (position[None, :] < count_at[:, None]).astype(jnp.float32) * live_slot[
        :, None
    ].astype(jnp.float32)
    weight_rows = residual[None, :] * live_rows

    def masked_block(operand):
        second_slot, live = operand
        right = lax.dynamic_slice_in_dim(gathered, second_slot * BLOCK, BLOCK, 1)
        right_sq = right * right
        return (right_sq.astype(jnp.float32) * live[:, None]).astype(jnp.bfloat16)

    masked = lax.map(masked_block, (second_at, live_rows))
    rows = BLOCK // shards

    def one_slot(slot, buffer):
        first_col = lax.dynamic_index_in_dim(first_at, slot, 0, keepdims=False) * BLOCK
        second_col = lax.dynamic_index_in_dim(second_at, slot, 0, keepdims=False) * BLOCK
        left = lax.dynamic_slice_in_dim(gathered, first_col, rows * lax.axis_size("samp"), 1)
        right = lax.dynamic_slice_in_dim(gathered, second_col, BLOCK, 1)
        row_weight = lax.dynamic_index_in_dim(weight_rows, slot, 0, keepdims=False)
        masked_slot = lax.dynamic_index_in_dim(masked, slot, 0, keepdims=False)
        weighted = (left.astype(jnp.float32) * row_weight[:, None]).astype(jnp.bfloat16)
        left_sq = left * left
        cross = jnp.einsum("si,sj->ij", weighted, right, preferred_element_type=jnp.float32)
        moment = jnp.einsum("si,sj->ij", left_sq, masked_slot, preferred_element_type=jnp.float32)
        stacked = jnp.stack([cross, moment], axis=1)[:, :, None, :]
        return lax.dynamic_update_slice_in_dim(buffer, stacked, slot, 2)

    start_buffer = jnp.zeros((rows * lax.axis_size("samp"), 2, width_slots, BLOCK), jnp.float32)
    shares = lax.psum_scatter(
        lax.fori_loop(0, width_slots, one_slot, start_buffer),
        "samp",
        scatter_dimension=0,
        tiled=True,
    )
    zvalue = shares[:, 0] / jnp.sqrt(spread_var * shares[:, 1] + 1e-06)
    row_sums = jnp.sum(zvalue, axis=2)
    col_sums = jnp.sum(zvalue, axis=0)
    live_float = live_slot.astype(jnp.float32)
    first_hot = (first_at[:, None] == block_ids[None, :]).astype(jnp.float32) * live_float[:, None]
    second_hot = (second_at[:, None] == block_ids[None, :]).astype(jnp.float32) * live_float[
        :, None
    ]
    by_column = jnp.dot(second_hot.T, col_sums, precision=highest)
    by_row = jnp.dot(first_hot.T, row_sums.T, precision=highest)
    row_start = lax.axis_index("samp") * rows
    placed = lax.dynamic_update_slice_in_dim(
        jnp.zeros((blocks, BLOCK), jnp.float32), by_row, row_start, 1
    )
    partial_scores = (by_column + placed).reshape(blocks * BLOCK)
    group_part = lax.psum_scatter(partial_scores, "snp", scatter_dimension=0, tiled=True)
    totals = lax.psum(group_part, "samp")
    return totals / math.sqrt(2 * BLOCK)


CHUNKS = 2
OFFSETS = [(dy, dz, dx, dc) for dy in range(2) for dz in range(4) for dx in range(2) for dc in range(2)]


def flip(bit, change):
    return 1 - bit if change else bit


def two_groups_kernel(
    list_ref, slot_ref, count_ref, dos_ref, res_ref, out_ref,
    mine, other, weights, square_sum, cross, moment, moment_half, cross_in, moment_in, final, send_vec,
    local_sem, mate_sem, mate_send, far_sem, far_send, res_sem, res_send,
    sum_sem, sum_send, cross_sem, cross_send, moment_sem, moment_send, final_sem, final_send,
):
    y = lax.axis_index("snp")
    k = lax.axis_index("samp")
    z, x, c = k // 4, (k // 2) % 2, k % 2
    rows = dos_ref.shape[0]
    part = rows // CHUNKS
    own = c + y - 2 * c * y
    share = BLOCK // 8

    def at(dy, dz, dx, dc):
        return (flip(y, dy), ((z + dz) % 4 * 2 + flip(x, dx)) * 2 + flip(c, dc))

    def column(block):
        return pl.ds(pl.multiple_of(block * BLOCK, BLOCK), BLOCK)

    def remote(src, dst, send, recv, to):
        copy = pltpu.make_async_remote_copy(
            src_ref=src, dst_ref=dst, send_sem=send, recv_sem=recv,
            device_id=to, device_id_type=pl.DeviceIdType.MESH,
        )
        copy.start()
        return copy

    local = pltpu.make_async_copy(dos_ref.at[:, column(own)], mine.at[0], local_sem)
    local.start()
    barrier = pltpu.get_barrier_semaphore()
    for offset in OFFSETS[1:]:
        pl.semaphore_signal(
            barrier, inc=1, device_id=at(*offset), device_id_type=pl.DeviceIdType.MESH
        )
    pl.semaphore_wait(barrier, len(OFFSETS) - 1)

    far = []
    for dc in range(2):
        for part_id in range(CHUNKS):
            span = pl.ds(part_id * part, part)
            far.append(
                remote(
                    dos_ref.at[span, column(flip(c, dc))], other.at[dc, span],
                    far_send.at[dc, part_id], far_sem.at[dc, part_id], at(1, 0, 0, dc),
                )
            )
    near = [
        remote(res_ref, weights, res_send, res_sem, at(0, 0, 0, 1)),
        remote(dos_ref.at[:, column(1 - own)], mine.at[1], mate_send, mate_sem, at(0, 0, 0, 1)),
    ]

    own_slot, far_slot = 2 * y + own, 2 * (1 - y) + c
    count = jnp.int32(0)
    for pair in range(4):
        first = slot_ref[list_ref[pair, 0]]
        second = slot_ref[list_ref[pair, 1]]
        here = ((first == own_slot) & (second == far_slot)) | (
            (first == far_slot) & (second == own_slot)
        )
        count = count + jnp.where(here, count_ref[pair], 0)
    hot_group = jnp.where(slot_ref[list_ref[0, 0]] >= 2, 1, 0)
    hot_here = jnp.where(hot_group == y, 1, 0)

    def products(dc, part_id):
        span = pl.ds(part_id * part, part)
        near_block = mine[dc, span, :]
        far_block = other[dc, span, :]
        pick = jnp.full((part, BLOCK), hot_here, jnp.int32) == 1
        left = jnp.where(pick, near_block, far_block).T
        right = jnp.where(pick, far_block, near_block)
        base = (k - c + flip(c, dc)) * rows + part_id * part
        live = (base + lax.broadcasted_iota(jnp.int32, (1, part), 1) < count).astype(jnp.float32)
        source = res_ref if dc == 0 else weights
        weight = source[:, span] * live
        left_wide = left.astype(jnp.float32)
        weighted = (left_wide * weight).astype(jnp.bfloat16)
        left_sq = (left_wide * left_wide).astype(jnp.bfloat16)
        masked = (left_sq.astype(jnp.float32) * live).astype(jnp.bfloat16)
        right_wide = right.astype(jnp.float32)
        right_sq = (right_wide * right_wide).astype(jnp.bfloat16)
        return (
            jnp.dot(weighted, right, preferred_element_type=jnp.float32),
            jnp.dot(masked, right_sq, preferred_element_type=jnp.float32),
        )

    local.wait()
    near[0].wait()
    both = res_ref[...] * res_ref[...] + weights[...] * weights[...]
    square_sum[0] = jnp.broadcast_to(jnp.sum(both, axis=1, keepdims=True), (8, 128))
    ring = [offset for offset in OFFSETS[1:] if offset[0] == 0 and offset[3] == 0]
    started = []
    for place, offset in enumerate(ring):
        started.append(
            remote(
                square_sum.at[0], square_sum.at[place + 1],
                sum_send.at[place], sum_sem.at[place], at(*offset),
            )
        )
    step = 0
    for dc in range(2):
        if dc == 1:
            near[1].wait()
        for part_id in range(CHUNKS):
            far[step].wait()
            cross_part, moment_part = products(dc, part_id)
            if step == 0:
                cross[...] = cross_part
                moment[...] = moment_part
            else:
                cross[...] += cross_part
                moment[...] += moment_part
            step += 1
    moment_half[...] = moment[...].astype(jnp.bfloat16)

    def share_of(place):
        return pl.ds(pl.multiple_of(place * share, share), share)

    for place, offset in enumerate(ring):
        to = at(*offset)
        span = share_of(to[1] // 2)
        started.append(
            remote(
                cross.at[span], cross_in.at[place],
                cross_send.at[place], cross_sem.at[place], to,
            )
        )
        started.append(
            remote(
                moment_half.at[span], moment_in.at[place],
                moment_send.at[place], moment_sem.at[place], to,
            )
        )
    for copy in started:
        copy.wait()
    span = share_of(k // 2)
    cross_sum = cross[span, :]
    moment_sum = moment[span, :]
    squares = square_sum[0]
    for place in range(len(ring)):
        cross_sum += cross_in[place]
        moment_sum += moment_in[place].astype(jnp.float32)
        squares += square_sum[place + 1]
    spread_var = squares[0:1, 0:1] / (rows * 16)
    zvalue = cross_sum / jnp.sqrt(spread_var * moment_sum + 1e-06)
    row_sums = jnp.sum(zvalue, axis=1, keepdims=True)
    col_vec = jnp.sum(zvalue, axis=0, keepdims=True)
    row_at = lax.broadcasted_iota(jnp.int32, (share, BLOCK), 0) + share * (k // 2)
    spot = row_at == lax.broadcasted_iota(jnp.int32, (share, BLOCK), 1)
    row_vec = jnp.sum(jnp.where(spot, row_sums, 0.0), axis=0, keepdims=True)
    pick_row = jnp.full((1, BLOCK), hot_here, jnp.int32) == 1
    send_vec[0] = jnp.where(pick_row, row_vec, col_vec)
    send_vec[1] = jnp.where(pick_row, col_vec, row_vec)
    started = []
    for place, offset in enumerate(OFFSETS):
        if place > 0:
            started.append(
                remote(
                    send_vec.at[offset[0]], final.at[place],
                    final_send.at[place], final_sem.at[place], at(*offset),
                )
            )
    final[0] = send_vec[0]
    for copy in started:
        copy.wait()
    total = {}
    for place, offset in enumerate(OFFSETS):
        key = (offset[0], offset[3])
        total[key] = total[key] + final[place] if key in total else final[place]
    swap_far = jnp.full((1, BLOCK), c, jnp.int32) == 1
    swap_own = jnp.full((1, BLOCK), own, jnp.int32) == 1
    scale = 1.0 / math.sqrt(2 * BLOCK)
    for block in range(2):
        same = jnp.where(swap_own, total[0, 1 - block], total[0, block])
        cross_group = jnp.where(swap_far, total[1, 1 - block], total[1, block])
        out_ref[block : block + 1, :] = (same + cross_group) * scale


def two_groups(dosages, residual, pair_list, block_slot, pair_counts):
    rows = dosages.shape[0]
    dma = pltpu.SemaphoreType.DMA
    peers = len(OFFSETS)
    smem = pl.BlockSpec(memory_space=pltpu.SMEM)
    vmem = pl.BlockSpec(memory_space=pltpu.VMEM)
    score = pl.pallas_call(
        two_groups_kernel,
        out_shape=jax.ShapeDtypeStruct((2, BLOCK), jnp.float32),
        in_specs=[smem, smem, smem, pl.BlockSpec(memory_space=pl.ANY), vmem],
        out_specs=vmem,
        scratch_shapes=[
            pltpu.VMEM((2, rows, BLOCK), jnp.bfloat16),
            pltpu.VMEM((2, rows, BLOCK), jnp.bfloat16),
            pltpu.VMEM((1, rows), jnp.float32),
            pltpu.VMEM((8, 8, 128), jnp.float32),
            pltpu.VMEM((BLOCK, BLOCK), jnp.float32),
            pltpu.VMEM((BLOCK, BLOCK), jnp.float32),
            pltpu.VMEM((BLOCK, BLOCK), jnp.bfloat16),
            pltpu.VMEM((7, BLOCK // 8, BLOCK), jnp.float32),
            pltpu.VMEM((7, BLOCK // 8, BLOCK), jnp.bfloat16),
            pltpu.VMEM((peers, 1, BLOCK), jnp.float32),
            pltpu.VMEM((2, 1, BLOCK), jnp.float32),
            dma, dma, dma, dma((2, CHUNKS)), dma((2, CHUNKS)), dma, dma,
            dma((7,)), dma((7,)), dma((7,)), dma((7,)), dma((7,)), dma((7,)),
            dma((peers,)), dma((peers,)),
        ],
        compiler_params=pltpu.CompilerParams(
            collective_id=0, has_side_effects=True, vmem_limit_bytes=32 * 1024 * 1024
        ),
        name="pair_scores",
    )(pair_list, block_slot, pair_counts, dosages, residual.reshape(1, rows))
    return score.reshape(2 * BLOCK)


def solution(mesh):
    def on_device(dosages, residual, pair_list, block_slot, pair_counts):
        groups, shards = lax.axis_size("snp"), lax.axis_size("samp")
        fits = groups == 2 and shards == 16 and block_slot.shape[0] == 4
        run = two_groups if fits else any_groups
        return run(dosages, residual, pair_list, block_slot, pair_counts)

    return jax.shard_map(
        on_device,
        mesh=mesh,
        in_specs=(P("samp", "snp"), P("samp"), P(), P(), P()),
        out_specs=P("snp"),
        check_vma=False,
    )
```

```python
import math

import jax
import jax.numpy as jnp
from jax import lax
from jax.experimental import pallas as pl
from jax.experimental.pallas import tpu as pltpu
from jax.sharding import PartitionSpec as P

BLOCK = 256


def any_groups(dosages, residual, pair_list, block_slot, pair_counts):
    local_rows = dosages.shape[0]
    groups = lax.axis_size("snp")
    shards = lax.axis_size("samp")
    total_rows = local_rows * shards
    blocks = block_slot.shape[0]
    num_pairs = pair_list.shape[0]
    highest = lax.Precision.HIGHEST
    gathered = lax.all_gather(dosages, "snp", axis=1, tiled=True)
    spread_sum = lax.psum(jnp.sum(residual * residual), "samp")
    spread_var = spread_sum / total_rows
    position = lax.axis_index("samp") * local_rows + jnp.arange(local_rows, dtype=jnp.int32)
    block_ids = jnp.arange(blocks, dtype=jnp.int32)
    slot_first = jnp.sum(
        (pair_list[:, 0:1] == block_ids[None, :]).astype(jnp.int32) * block_slot[None, :], axis=1
    )
    slot_second = jnp.sum(
        (pair_list[:, 1:2] == block_ids[None, :]).astype(jnp.int32) * block_slot[None, :], axis=1
    )
    group_id = lax.axis_index("snp")
    pair_ids = jnp.arange(num_pairs, dtype=jnp.int32)
    width_slots = (num_pairs + groups - 1) // groups
    wanted = group_id * width_slots + jnp.arange(width_slots, dtype=jnp.int32)
    picked = (pair_ids[:, None] == wanted[None, :]).astype(jnp.int32)
    live_slot = jnp.sum(picked, axis=0)
    first_at = jnp.sum(picked * slot_first[:, None], axis=0)
    second_at = jnp.sum(picked * slot_second[:, None], axis=0)
    count_at = jnp.sum(picked * pair_counts[:, None], axis=0)
    live_rows = (position[None, :] < count_at[:, None]).astype(jnp.float32) * live_slot[
        :, None
    ].astype(jnp.float32)
    weight_rows = residual[None, :] * live_rows

    def masked_block(operand):
        second_slot, live = operand
        right = lax.dynamic_slice_in_dim(gathered, second_slot * BLOCK, BLOCK, 1)
        right_sq = right * right
        return (right_sq.astype(jnp.float32) * live[:, None]).astype(jnp.bfloat16)

    masked = lax.map(masked_block, (second_at, live_rows))
    rows = BLOCK // shards

    def one_slot(slot, buffer):
        first_col = lax.dynamic_index_in_dim(first_at, slot, 0, keepdims=False) * BLOCK
        second_col = lax.dynamic_index_in_dim(second_at, slot, 0, keepdims=False) * BLOCK
        left = lax.dynamic_slice_in_dim(gathered, first_col, rows * lax.axis_size("samp"), 1)
        right = lax.dynamic_slice_in_dim(gathered, second_col, BLOCK, 1)
        row_weight = lax.dynamic_index_in_dim(weight_rows, slot, 0, keepdims=False)
        masked_slot = lax.dynamic_index_in_dim(masked, slot, 0, keepdims=False)
        weighted = (left.astype(jnp.float32) * row_weight[:, None]).astype(jnp.bfloat16)
        left_sq = left * left
        cross = jnp.einsum("si,sj->ij", weighted, right, preferred_element_type=jnp.float32)
        moment = jnp.einsum("si,sj->ij", left_sq, masked_slot, preferred_element_type=jnp.float32)
        stacked = jnp.stack([cross, moment], axis=1)[:, :, None, :]
        return lax.dynamic_update_slice_in_dim(buffer, stacked, slot, 2)

    start_buffer = jnp.zeros((rows * lax.axis_size("samp"), 2, width_slots, BLOCK), jnp.float32)
    shares = lax.psum_scatter(
        lax.fori_loop(0, width_slots, one_slot, start_buffer),
        "samp",
        scatter_dimension=0,
        tiled=True,
    )
    zvalue = shares[:, 0] / jnp.sqrt(spread_var * shares[:, 1] + 1e-06)
    row_sums = jnp.sum(zvalue, axis=2)
    col_sums = jnp.sum(zvalue, axis=0)
    live_float = live_slot.astype(jnp.float32)
    first_hot = (first_at[:, None] == block_ids[None, :]).astype(jnp.float32) * live_float[:, None]
    second_hot = (second_at[:, None] == block_ids[None, :]).astype(jnp.float32) * live_float[
        :, None
    ]
    by_column = jnp.dot(second_hot.T, col_sums, precision=highest)
    by_row = jnp.dot(first_hot.T, row_sums.T, precision=highest)
    row_start = lax.axis_index("samp") * rows
    placed = lax.dynamic_update_slice_in_dim(
        jnp.zeros((blocks, BLOCK), jnp.float32), by_row, row_start, 1
    )
    partial_scores = (by_column + placed).reshape(blocks * BLOCK)
    group_part = lax.psum_scatter(partial_scores, "snp", scatter_dimension=0, tiled=True)
    totals = lax.psum(group_part, "samp")
    return totals / math.sqrt(2 * BLOCK)


HALVES = 2
RING = [(0, dz, dx, 0) for dz in range(4) for dx in range(2)][1:]
COLUMN = [(0, 0, 0, 1), (1, 0, 0, 0), (1, 0, 0, 1)]


def flip(bit, change):
    return 1 - bit if change else bit


def two_groups_kernel(
    list_hbm, slot_hbm, count_hbm, dos_ref, res_ref, out_ref,
    list_ref, slot_ref, count_ref, mine, other, residuals, left_weighted, left_masked, right_weight,
    square_sum, cross, moment, parts, parts_in, vecs, vecs_in, last, last_in,
    local_sem, mate_sem, mate_send, far_sem, far_send, res_sem, res_send,
    sum_sem, sum_send, part_sem, part_send, vec_sem, vec_send, last_sem, last_send,
):
    y = lax.axis_index("snp")
    k = lax.axis_index("samp")
    z, x, c = k // 4, (k // 2) % 2, k % 2
    rows = dos_ref.shape[0]
    own = c + y - 2 * c * y
    share = BLOCK // 8
    width = BLOCK // HALVES
    mesh_id = pl.DeviceIdType.MESH

    def at(dy, dz, dx, dc):
        return (flip(y, dy), ((z + dz) % 4 * 2 + flip(x, dx)) * 2 + flip(c, dc))

    def column(start, size):
        return pl.ds(pl.multiple_of(start, 128), size)

    def remote(src, dst, send, recv, to):
        copy = pltpu.make_async_remote_copy(
            src_ref=src, dst_ref=dst, send_sem=send, recv_sem=recv,
            device_id=to, device_id_type=mesh_id,
        )
        copy.start()
        return copy

    barrier = pltpu.get_barrier_semaphore()
    for offset in COLUMN + RING:
        pl.semaphore_signal(barrier, inc=1, device_id=at(*offset), device_id_type=mesh_id)
    local = [
        pltpu.make_async_copy(dos_ref.at[:, column(own * BLOCK, BLOCK)], mine.at[0], local_sem.at[0]),
        pltpu.make_async_copy(res_ref, residuals.at[0, 0], local_sem.at[1]),
        pltpu.make_async_copy(list_hbm, list_ref, local_sem.at[2]),
        pltpu.make_async_copy(slot_hbm, slot_ref, local_sem.at[3]),
        pltpu.make_async_copy(count_hbm, count_ref, local_sem.at[4]),
    ]
    for copy in local:
        copy.start()
    pl.semaphore_wait(barrier, len(COLUMN + RING))

    far = []
    for half in range(HALVES):
        for dc in range(2):
            far.append(
                remote(
                    dos_ref.at[:, column(flip(c, dc) * BLOCK + half * width, width)],
                    other.at[half, dc],
                    far_send.at[half, dc], far_sem.at[half, dc], at(1, 0, 0, dc),
                )
            )
    mate_res = remote(res_ref, residuals.at[1, 0], res_send, res_sem, at(0, 0, 0, 1))
    mate_block = remote(
        dos_ref.at[:, column((1 - own) * BLOCK, BLOCK)], mine.at[1], mate_send, mate_sem, at(0, 0, 0, 1)
    )
    for copy in local:
        copy.wait()

    own_slot, far_slot = 2 * y + own, 2 * (1 - y) + c
    count = jnp.int32(0)
    for pair in range(4):
        first = slot_ref[list_ref[0, pair]]
        second = slot_ref[list_ref[1, pair]]
        here = ((first == own_slot) & (second == far_slot)) | (
            (first == far_slot) & (second == own_slot)
        )
        count = count + jnp.where(here, count_ref[pair], 0)
    hot_group = jnp.where(slot_ref[list_ref[0, 0]] >= 2, 1, 0)
    hot_here = jnp.where(hot_group == y, 1, 0)

    mate_res.wait()
    both = residuals[0] * residuals[0] + residuals[1] * residuals[1]
    square_sum[0] = jnp.broadcast_to(jnp.sum(both, axis=1, keepdims=True), (8, 128))
    started = []
    for place, offset in enumerate(RING):
        started.append(
            remote(
                square_sum.at[0], square_sum.at[place + 1],
                sum_send.at[place], sum_sem.at[place], at(*offset),
            )
        )
    for dc in range(2):
        if dc == 1:
            mate_block.wait()
        base = (k - c + flip(c, dc)) * rows
        live = (base + lax.broadcasted_iota(jnp.int32, (1, rows), 1) < count).astype(jnp.float32)
        pick = jnp.full((1, rows), hot_here, jnp.int32) == 1
        weight = residuals[dc]
        left = mine[dc].T.astype(jnp.float32)
        left_weighted[dc] = (left * (jnp.where(pick, weight, 1.0) * live)).astype(jnp.bfloat16)
        left_sq = (left * left).astype(jnp.bfloat16).astype(jnp.float32)
        left_masked[dc] = (left_sq * live).astype(jnp.bfloat16)
        right_weight[dc] = jnp.broadcast_to(jnp.where(pick, 1.0, weight), (width, rows)).T
    for half in range(HALVES):
        for dc in range(2):
            far[2 * half + dc].wait()
            right = other[half, dc].astype(jnp.float32)
            weighted = (right * right_weight[dc]).astype(jnp.bfloat16)
            squares = (right * right).astype(jnp.bfloat16)
            cross_part = jnp.dot(left_weighted[dc], weighted, preferred_element_type=jnp.float32)
            moment_part = jnp.dot(left_masked[dc], squares, preferred_element_type=jnp.float32)
            if dc == 0:
                cross[half] = cross_part.reshape(8, share, width)
                moment[half] = moment_part.reshape(8, share, width)
            else:
                cross_all = cross[half] + cross_part.reshape(8, share, width)
                moment_all = moment[half] + moment_part.reshape(8, share, width)
                cross[half] = cross_all
                moment[half] = moment_all
                parts[half, :, :share, :] = cross_all.astype(jnp.bfloat16)
                parts[half, :, share:, :] = moment_all.astype(jnp.bfloat16)
        for place, offset in enumerate(RING):
            to = at(*offset)
            started.append(
                remote(
                    parts.at[half, to[1] // 2], parts_in.at[half, place],
                    part_send.at[half, place], part_sem.at[half, place], to,
                )
            )
    for copy in started[: len(RING)]:
        copy.wait()
    total = square_sum[0]
    for place in range(len(RING)):
        total += square_sum[place + 1]
    spread_var = total[0:1, 0:1] / (rows * 16)
    row_sums = jnp.zeros((share, 1), jnp.float32)
    for half in range(HALVES):
        cross_sum = cross[half, k // 2]
        moment_sum = moment[half, k // 2]
        for place in range(len(RING)):
            started[(1 + half) * len(RING) + place].wait()
            cross_sum += parts_in[half, place, :share, :].astype(jnp.float32)
            moment_sum += parts_in[half, place, share:, :].astype(jnp.float32)
        zvalue = cross_sum / jnp.sqrt(spread_var * moment_sum + 1e-06)
        row_sums += jnp.sum(zvalue, axis=1, keepdims=True)
        vecs[1, :, half * width : (half + 1) * width] = jnp.sum(zvalue, axis=0, keepdims=True)
    row_at = lax.broadcasted_iota(jnp.int32, (share, BLOCK), 0) + share * (k // 2)
    spot = row_at == lax.broadcasted_iota(jnp.int32, (share, BLOCK), 1)
    vecs[0] = jnp.sum(jnp.where(spot, row_sums, 0.0), axis=0, keepdims=True)
    started = []
    for place, offset in enumerate(RING):
        started.append(
            remote(vecs, vecs_in.at[place], vec_send.at[place], vec_sem.at[place], at(*offset))
        )
    total = vecs[...]
    for place in range(len(RING)):
        started[place].wait()
        total += vecs_in[place]
    last[...] = total
    started = []
    for place, offset in enumerate(COLUMN):
        started.append(
            remote(
                last.at[offset[0]], last_in.at[place],
                last_send.at[place], last_sem.at[place], at(*offset),
            )
        )
    for copy in started:
        copy.wait()
    swap_far = jnp.full((1, BLOCK), c, jnp.int32) == 1
    swap_own = jnp.full((1, BLOCK), own, jnp.int32) == 1
    by_own = [last[0], last_in[0]]
    by_far = [last_in[1], last_in[2]]
    scale = 1.0 / math.sqrt(2 * BLOCK)
    for block in range(2):
        same = jnp.where(swap_own, by_own[1 - block], by_own[block])
        cross_group = jnp.where(swap_far, by_far[1 - block], by_far[block])
        out_ref[block : block + 1, :] = (same + cross_group) * scale


def two_groups(dosages, residual, pair_list, block_slot, pair_counts):
    rows = dosages.shape[0]
    width = BLOCK // HALVES
    dma = pltpu.SemaphoreType.DMA
    peers = len(RING)
    hbm = pl.BlockSpec(memory_space=pltpu.HBM)
    half_type, full_type = jnp.bfloat16, jnp.float32
    score = pl.pallas_call(
        two_groups_kernel,
        out_shape=jax.ShapeDtypeStruct((2, BLOCK), jnp.float32),
        in_specs=[hbm, hbm, hbm, hbm, hbm],
        out_specs=pl.BlockSpec(memory_space=pltpu.VMEM),
        scratch_shapes=[
            pltpu.SMEM((2, 4), jnp.int32),
            pltpu.SMEM((4,), jnp.int32),
            pltpu.SMEM((4,), jnp.int32),
            pltpu.VMEM((2, rows, BLOCK), half_type),
            pltpu.VMEM((HALVES, 2, rows, width), half_type),
            pltpu.VMEM((2, 1, rows), full_type),
            pltpu.VMEM((2, BLOCK, rows), half_type),
            pltpu.VMEM((2, BLOCK, rows), half_type),
            pltpu.VMEM((2, rows, width), full_type),
            pltpu.VMEM((peers + 1, 8, 128), full_type),
            pltpu.VMEM((HALVES, 8, BLOCK // 8, width), full_type),
            pltpu.VMEM((HALVES, 8, BLOCK // 8, width), full_type),
            pltpu.VMEM((HALVES, 8, BLOCK // 4, width), half_type),
            pltpu.VMEM((HALVES, peers, BLOCK // 4, width), half_type),
            pltpu.VMEM((2, 1, BLOCK), full_type),
            pltpu.VMEM((peers, 2, 1, BLOCK), full_type),
            pltpu.VMEM((2, 1, BLOCK), full_type),
            pltpu.VMEM((3, 1, BLOCK), full_type),
            dma((5,)), dma, dma, dma((HALVES, 2)), dma((HALVES, 2)), dma, dma,
            dma((peers,)), dma((peers,)), dma((HALVES, peers)), dma((HALVES, peers)),
            dma((peers,)), dma((peers,)), dma((3,)), dma((3,)),
        ],
        compiler_params=pltpu.CompilerParams(
            collective_id=0, has_side_effects=True, vmem_limit_bytes=32 * 1024 * 1024
        ),
        name="pair_scores",
    )(pair_list.T, block_slot, pair_counts, dosages, residual)
    return score.reshape(2 * BLOCK)


def solution(mesh):
    def on_device(dosages, residual, pair_list, block_slot, pair_counts):
        groups, shards = lax.axis_size("snp"), lax.axis_size("samp")
        fits = groups == 2 and shards == 16 and block_slot.shape[0] == 4
        run = two_groups if fits else any_groups
        return run(dosages, residual, pair_list, block_slot, pair_counts)

    return jax.shard_map(
        on_device,
        mesh=mesh,
        in_specs=(P("samp", "snp"), P("samp"), P(), P(), P()),
        out_specs=P("snp"),
        check_vma=False,
    )
```

```python
import math

import jax
import jax.numpy as jnp
from jax import lax
from jax.experimental import pallas as pl
from jax.experimental.pallas import tpu as pltpu
from jax.sharding import PartitionSpec as P

BLOCK = 256


def any_groups(dosages, residual, pair_list, block_slot, pair_counts):
    local_rows = dosages.shape[0]
    groups = lax.axis_size("snp")
    shards = lax.axis_size("samp")
    total_rows = local_rows * shards
    blocks = block_slot.shape[0]
    num_pairs = pair_list.shape[0]
    highest = lax.Precision.HIGHEST
    gathered = lax.all_gather(dosages, "snp", axis=1, tiled=True)
    spread_sum = lax.psum(jnp.sum(residual * residual), "samp")
    spread_var = spread_sum / total_rows
    position = lax.axis_index("samp") * local_rows + jnp.arange(local_rows, dtype=jnp.int32)
    block_ids = jnp.arange(blocks, dtype=jnp.int32)
    slot_first = jnp.sum(
        (pair_list[:, 0:1] == block_ids[None, :]).astype(jnp.int32) * block_slot[None, :], axis=1
    )
    slot_second = jnp.sum(
        (pair_list[:, 1:2] == block_ids[None, :]).astype(jnp.int32) * block_slot[None, :], axis=1
    )
    group_id = lax.axis_index("snp")
    pair_ids = jnp.arange(num_pairs, dtype=jnp.int32)
    width_slots = (num_pairs + groups - 1) // groups
    wanted = group_id * width_slots + jnp.arange(width_slots, dtype=jnp.int32)
    picked = (pair_ids[:, None] == wanted[None, :]).astype(jnp.int32)
    live_slot = jnp.sum(picked, axis=0)
    first_at = jnp.sum(picked * slot_first[:, None], axis=0)
    second_at = jnp.sum(picked * slot_second[:, None], axis=0)
    count_at = jnp.sum(picked * pair_counts[:, None], axis=0)
    live_rows = (position[None, :] < count_at[:, None]).astype(jnp.float32) * live_slot[
        :, None
    ].astype(jnp.float32)
    weight_rows = residual[None, :] * live_rows

    def masked_block(operand):
        second_slot, live = operand
        right = lax.dynamic_slice_in_dim(gathered, second_slot * BLOCK, BLOCK, 1)
        right_sq = right * right
        return (right_sq.astype(jnp.float32) * live[:, None]).astype(jnp.bfloat16)

    masked = lax.map(masked_block, (second_at, live_rows))
    rows = BLOCK // shards

    def one_slot(slot, buffer):
        first_col = lax.dynamic_index_in_dim(first_at, slot, 0, keepdims=False) * BLOCK
        second_col = lax.dynamic_index_in_dim(second_at, slot, 0, keepdims=False) * BLOCK
        left = lax.dynamic_slice_in_dim(gathered, first_col, rows * lax.axis_size("samp"), 1)
        right = lax.dynamic_slice_in_dim(gathered, second_col, BLOCK, 1)
        row_weight = lax.dynamic_index_in_dim(weight_rows, slot, 0, keepdims=False)
        masked_slot = lax.dynamic_index_in_dim(masked, slot, 0, keepdims=False)
        weighted = (left.astype(jnp.float32) * row_weight[:, None]).astype(jnp.bfloat16)
        left_sq = left * left
        cross = jnp.einsum("si,sj->ij", weighted, right, preferred_element_type=jnp.float32)
        moment = jnp.einsum("si,sj->ij", left_sq, masked_slot, preferred_element_type=jnp.float32)
        stacked = jnp.stack([cross, moment], axis=1)[:, :, None, :]
        return lax.dynamic_update_slice_in_dim(buffer, stacked, slot, 2)

    start_buffer = jnp.zeros((rows * lax.axis_size("samp"), 2, width_slots, BLOCK), jnp.float32)
    shares = lax.psum_scatter(
        lax.fori_loop(0, width_slots, one_slot, start_buffer),
        "samp",
        scatter_dimension=0,
        tiled=True,
    )
    zvalue = shares[:, 0] / jnp.sqrt(spread_var * shares[:, 1] + 1e-06)
    row_sums = jnp.sum(zvalue, axis=2)
    col_sums = jnp.sum(zvalue, axis=0)
    live_float = live_slot.astype(jnp.float32)
    first_hot = (first_at[:, None] == block_ids[None, :]).astype(jnp.float32) * live_float[:, None]
    second_hot = (second_at[:, None] == block_ids[None, :]).astype(jnp.float32) * live_float[
        :, None
    ]
    by_column = jnp.dot(second_hot.T, col_sums, precision=highest)
    by_row = jnp.dot(first_hot.T, row_sums.T, precision=highest)
    row_start = lax.axis_index("samp") * rows
    placed = lax.dynamic_update_slice_in_dim(
        jnp.zeros((blocks, BLOCK), jnp.float32), by_row, row_start, 1
    )
    partial_scores = (by_column + placed).reshape(blocks * BLOCK)
    group_part = lax.psum_scatter(partial_scores, "snp", scatter_dimension=0, tiled=True)
    totals = lax.psum(group_part, "samp")
    return totals / math.sqrt(2 * BLOCK)


HALVES = 2
RING = [(0, dz, dx, 0) for dz in range(4) for dx in range(2)][1:]
COLUMN = [(0, 0, 0, 1), (1, 0, 0, 0), (1, 0, 0, 1)]
CHIPS = [(dy, dz, dx, 0) for dy in range(2) for dz in range(4) for dx in range(2)][1:]


def flip(bit, change):
    return 1 - bit if change else bit


def two_groups_kernel(
    list_hbm, slot_hbm, count_hbm, dos_ref, res_ref, out_ref,
    list_ref, slot_ref, count_ref, mine, other, residuals, left_weighted, left_masked, right_weight,
    square_sum, cross, moment, parts, parts_in, vecs, vecs_in, chip, chip_in,
    local_sem, mate_sem, mate_send, far_sem, far_send, res_sem, res_send,
    sum_sem, sum_send, part_sem, part_send, vec_sem, vec_send, chip_sem, chip_send, round_sem,
):
    y = lax.axis_index("snp")
    k = lax.axis_index("samp")
    z, x, c = k // 4, (k // 2) % 2, k % 2
    rows = dos_ref.shape[0]
    own = c + y - 2 * c * y
    share = BLOCK // 8
    width = BLOCK // HALVES
    mesh_id = pl.DeviceIdType.MESH

    def at(dy, dz, dx, dc):
        return (flip(y, dy), ((z + dz) % 4 * 2 + flip(x, dx)) * 2 + flip(c, dc))

    def column(start, size):
        return pl.ds(pl.multiple_of(start, 128), size)

    def remote(src, dst, send, recv, to):
        copy = pltpu.make_async_remote_copy(
            src_ref=src, dst_ref=dst, send_sem=send, recv_sem=recv,
            device_id=to, device_id_type=mesh_id,
        )
        copy.start()
        return copy

    def take(sem, like):
        pltpu.make_async_copy(like, like, sem).wait()

    def greet(sem, *offset):
        pl.semaphore_signal(sem, inc=1, device_id=at(*offset), device_id_type=mesh_id)

    def greet_neighbours(sem):
        greet(sem, 0, 0, 1, 0)

        @pl.when(z > 0)
        def _():
            greet(sem, 0, 3, 0, 0)

        @pl.when(z < 3)
        def _():
            greet(sem, 0, 1, 0, 0)

    neighbours = 1 + jnp.where(z > 0, 1, 0) + jnp.where(z < 3, 1, 0)
    barrier = pltpu.get_barrier_semaphore()
    for offset in COLUMN:
        greet(barrier, *offset)
    greet_neighbours(barrier)
    local = [
        pltpu.make_async_copy(dos_ref.at[:, column(own * BLOCK, BLOCK)], mine.at[0], local_sem.at[0]),
        pltpu.make_async_copy(res_ref, residuals.at[0, 0], local_sem.at[1]),
        pltpu.make_async_copy(list_hbm, list_ref, local_sem.at[2]),
        pltpu.make_async_copy(slot_hbm, slot_ref, local_sem.at[3]),
        pltpu.make_async_copy(count_hbm, count_ref, local_sem.at[4]),
    ]
    for copy in local:
        copy.start()
    pl.semaphore_wait(barrier, len(COLUMN) + neighbours)

    far = []
    for half in range(HALVES):
        for dc in range(2):
            far.append(
                remote(
                    dos_ref.at[:, column(flip(c, dc) * BLOCK + half * width, width)],
                    other.at[half, dc],
                    far_send.at[half, dc], far_sem.at[half, dc], at(1, 0, 0, dc),
                )
            )
    mate_res = remote(res_ref, residuals.at[1, 0], res_send, res_sem, at(0, 0, 0, 1))
    mate_block = remote(
        dos_ref.at[:, column((1 - own) * BLOCK, BLOCK)], mine.at[1], mate_send, mate_sem, at(0, 0, 0, 1)
    )
    greet_neighbours(round_sem.at[0])
    for copy in local:
        copy.wait()

    own_slot, far_slot = 2 * y + own, 2 * (1 - y) + c
    count = jnp.int32(0)
    for pair in range(4):
        first = slot_ref[list_ref[0, pair]]
        second = slot_ref[list_ref[1, pair]]
        here = ((first == own_slot) & (second == far_slot)) | (
            (first == far_slot) & (second == own_slot)
        )
        count = count + jnp.where(here, count_ref[pair], 0)
    hot_group = jnp.where(slot_ref[list_ref[0, 0]] >= 2, 1, 0)
    hot_here = jnp.where(hot_group == y, 1, 0)

    for dc in range(2):
        if dc == 1:
            pl.semaphore_wait(round_sem.at[0], neighbours)
            greet_neighbours(round_sem.at[1])
            mate_res.wait_recv()
            mate_block.wait_recv()
        base = (k - c + flip(c, dc)) * rows
        live = (base + lax.broadcasted_iota(jnp.int32, (1, rows), 1) < count).astype(jnp.float32)
        pick = jnp.full((1, rows), hot_here, jnp.int32) == 1
        weight = residuals[dc]
        left = mine[dc].T.astype(jnp.float32)
        left_weighted[dc] = (left * (jnp.where(pick, weight, 1.0) * live)).astype(jnp.bfloat16)
        left_sq = (left * left).astype(jnp.bfloat16).astype(jnp.float32)
        left_masked[dc] = (left_sq * live).astype(jnp.bfloat16)
        right_weight[dc] = jnp.broadcast_to(jnp.where(pick, 1.0, weight), (width, rows)).T
    pl.semaphore_wait(round_sem.at[1], neighbours)
    greet_neighbours(round_sem.at[2])
    pl.semaphore_wait(round_sem.at[2], neighbours)
    greet(round_sem.at[3], 1, 0, 0, 0)
    both = residuals[0] * residuals[0] + residuals[1] * residuals[1]
    square_sum[0] = jnp.broadcast_to(jnp.sum(both, axis=1, keepdims=True), (8, 128))
    for place, offset in enumerate(RING):
        remote(square_sum.at[0], square_sum.at[place + 1], sum_send, sum_sem, at(*offset))
    pl.semaphore_wait(round_sem.at[3], 1)
    for half in range(HALVES):
        for dc in range(2):
            far[2 * half + dc].wait_recv()
            right = other[half, dc].astype(jnp.float32)
            weighted = (right * right_weight[dc]).astype(jnp.bfloat16)
            squares = (right * right).astype(jnp.bfloat16)
            cross_part = jnp.dot(left_weighted[dc], weighted, preferred_element_type=jnp.float32)
            moment_part = jnp.dot(left_masked[dc], squares, preferred_element_type=jnp.float32)
            if dc == 0:
                cross[half] = cross_part.reshape(8, share, width)
                moment[half] = moment_part.reshape(8, share, width)
            else:
                cross_all = cross[half] + cross_part.reshape(8, share, width)
                moment_all = moment[half] + moment_part.reshape(8, share, width)
                cross[half] = cross_all
                moment[half] = moment_all
                parts[half, :, :share, :] = cross_all.astype(jnp.bfloat16)
                parts[half, :, share:, :] = moment_all.astype(jnp.bfloat16)
        for place, offset in enumerate(RING):
            to = at(*offset)
            remote(
                parts.at[half, to[1] // 2], parts_in.at[half, place],
                part_send.at[half], part_sem.at[half], to,
            )
    others = square_sum.at[pl.ds(1, len(RING))]
    take(sum_sem, others)
    total = square_sum[0]
    for place in range(len(RING)):
        total += square_sum[place + 1]
    spread_var = total[0:1, 0:1] / (rows * 16)
    row_sums = jnp.zeros((share, 1), jnp.float32)
    for half in range(HALVES):
        cross_sum = cross[half, k // 2]
        moment_sum = moment[half, k // 2]
        take(part_sem.at[half], parts_in.at[half])
        for place in range(len(RING)):
            cross_sum += parts_in[half, place, :share, :].astype(jnp.float32)
            moment_sum += parts_in[half, place, share:, :].astype(jnp.float32)
        zvalue = cross_sum / jnp.sqrt(spread_var * moment_sum + 1e-06)
        row_sums += jnp.sum(zvalue, axis=1, keepdims=True)
        vecs[1, :, half * width : (half + 1) * width] = jnp.sum(zvalue, axis=0, keepdims=True)
    row_at = lax.broadcasted_iota(jnp.int32, (share, BLOCK), 0) + share * (k // 2)
    spot = row_at == lax.broadcasted_iota(jnp.int32, (share, BLOCK), 1)
    vecs[0] = jnp.sum(jnp.where(spot, row_sums, 0.0), axis=0, keepdims=True)
    mate_vecs = remote(vecs, vecs_in, vec_send, vec_sem, at(0, 0, 0, 1))
    mate_vecs.wait_recv()
    for group, block_here in ((0, own), (1, c)):
        here, there = vecs[group], vecs_in[group]
        for block in range(2):
            pick = jnp.full((1, BLOCK), block_here, jnp.int32) == block
            chip[group, block : block + 1, :] = jnp.where(pick, here, there)
    for place, offset in enumerate(CHIPS):
        remote(chip.at[offset[0]], chip_in.at[place + 1], chip_send, chip_sem, at(*offset))
    chip_in[0] = chip[0]
    other_chips = chip_in.at[pl.ds(1, len(CHIPS))]
    take(chip_sem, other_chips)
    out_ref[...] = jnp.sum(chip_in[...], axis=0) * (1.0 / math.sqrt(2 * BLOCK))
    for copy in far + [mate_res, mate_block, mate_vecs]:
        copy.wait_send()
    take(sum_send, others)
    for half in range(HALVES):
        take(part_send.at[half], parts_in.at[half])
    take(chip_send, other_chips)


def two_groups(dosages, residual, pair_list, block_slot, pair_counts):
    rows = dosages.shape[0]
    width = BLOCK // HALVES
    dma = pltpu.SemaphoreType.DMA
    peers = len(RING)
    hbm = pl.BlockSpec(memory_space=pltpu.HBM)
    half_type, full_type = jnp.bfloat16, jnp.float32
    score = pl.pallas_call(
        two_groups_kernel,
        out_shape=jax.ShapeDtypeStruct((2, BLOCK), jnp.float32),
        in_specs=[hbm, hbm, hbm, hbm, hbm],
        out_specs=pl.BlockSpec(memory_space=pltpu.VMEM),
        scratch_shapes=[
            pltpu.SMEM((2, 4), jnp.int32),
            pltpu.SMEM((4,), jnp.int32),
            pltpu.SMEM((4,), jnp.int32),
            pltpu.VMEM((2, rows, BLOCK), half_type),
            pltpu.VMEM((HALVES, 2, rows, width), half_type),
            pltpu.VMEM((2, 1, rows), full_type),
            pltpu.VMEM((2, BLOCK, rows), half_type),
            pltpu.VMEM((2, BLOCK, rows), half_type),
            pltpu.VMEM((2, rows, width), full_type),
            pltpu.VMEM((peers + 1, 8, 128), full_type),
            pltpu.VMEM((HALVES, 8, BLOCK // 8, width), full_type),
            pltpu.VMEM((HALVES, 8, BLOCK // 8, width), full_type),
            pltpu.VMEM((HALVES, 8, BLOCK // 4, width), half_type),
            pltpu.VMEM((HALVES, peers, BLOCK // 4, width), half_type),
            pltpu.VMEM((2, 1, BLOCK), full_type),
            pltpu.VMEM((2, 1, BLOCK), full_type),
            pltpu.VMEM((2, 2, BLOCK), full_type),
            pltpu.VMEM((len(CHIPS) + 1, 2, BLOCK), full_type),
            dma((5,)), dma, dma, dma((HALVES, 2)), dma((HALVES, 2)), dma, dma,
            dma, dma, dma((HALVES,)), dma((HALVES,)), dma, dma, dma, dma,
            pltpu.SemaphoreType.REGULAR((4,)),
        ],
        compiler_params=pltpu.CompilerParams(
            collective_id=0, has_side_effects=True, vmem_limit_bytes=62 * 1024 * 1024
        ),
        name="pair_scores",
    )(pair_list.T, block_slot, pair_counts, dosages, residual)
    return score.reshape(2 * BLOCK)


def solution(mesh):
    def on_device(dosages, residual, pair_list, block_slot, pair_counts):
        groups, shards = lax.axis_size("snp"), lax.axis_size("samp")
        fits = groups == 2 and shards == 16 and block_slot.shape[0] == 4
        run = two_groups if fits else any_groups
        return run(dosages, residual, pair_list, block_slot, pair_counts)

    return jax.shard_map(
        on_device,
        mesh=mesh,
        in_specs=(P("samp", "snp"), P("samp"), P(), P(), P()),
        out_specs=P("snp"),
        check_vma=False,
    )
```

```python
import math

import jax
import jax.numpy as jnp
from jax import lax
from jax.experimental import pallas as pl
from jax.experimental.pallas import tpu as pltpu
from jax.sharding import PartitionSpec as P

BLOCK = 256


def any_groups(dosages, residual, pair_list, block_slot, pair_counts):
    local_rows = dosages.shape[0]
    groups = lax.axis_size("snp")
    shards = lax.axis_size("samp")
    total_rows = local_rows * shards
    blocks = block_slot.shape[0]
    num_pairs = pair_list.shape[0]
    highest = lax.Precision.HIGHEST
    gathered = lax.all_gather(dosages, "snp", axis=1, tiled=True)
    spread_sum = lax.psum(jnp.sum(residual * residual), "samp")
    spread_var = spread_sum / total_rows
    position = lax.axis_index("samp") * local_rows + jnp.arange(local_rows, dtype=jnp.int32)
    block_ids = jnp.arange(blocks, dtype=jnp.int32)
    slot_first = jnp.sum(
        (pair_list[:, 0:1] == block_ids[None, :]).astype(jnp.int32) * block_slot[None, :], axis=1
    )
    slot_second = jnp.sum(
        (pair_list[:, 1:2] == block_ids[None, :]).astype(jnp.int32) * block_slot[None, :], axis=1
    )
    group_id = lax.axis_index("snp")
    pair_ids = jnp.arange(num_pairs, dtype=jnp.int32)
    width_slots = (num_pairs + groups - 1) // groups
    wanted = group_id * width_slots + jnp.arange(width_slots, dtype=jnp.int32)
    picked = (pair_ids[:, None] == wanted[None, :]).astype(jnp.int32)
    live_slot = jnp.sum(picked, axis=0)
    first_at = jnp.sum(picked * slot_first[:, None], axis=0)
    second_at = jnp.sum(picked * slot_second[:, None], axis=0)
    count_at = jnp.sum(picked * pair_counts[:, None], axis=0)
    live_rows = (position[None, :] < count_at[:, None]).astype(jnp.float32) * live_slot[
        :, None
    ].astype(jnp.float32)
    weight_rows = residual[None, :] * live_rows

    def masked_block(operand):
        second_slot, live = operand
        right = lax.dynamic_slice_in_dim(gathered, second_slot * BLOCK, BLOCK, 1)
        right_sq = right * right
        return (right_sq.astype(jnp.float32) * live[:, None]).astype(jnp.bfloat16)

    masked = lax.map(masked_block, (second_at, live_rows))
    rows = BLOCK // shards

    def one_slot(slot, buffer):
        first_col = lax.dynamic_index_in_dim(first_at, slot, 0, keepdims=False) * BLOCK
        second_col = lax.dynamic_index_in_dim(second_at, slot, 0, keepdims=False) * BLOCK
        left = lax.dynamic_slice_in_dim(gathered, first_col, rows * lax.axis_size("samp"), 1)
        right = lax.dynamic_slice_in_dim(gathered, second_col, BLOCK, 1)
        row_weight = lax.dynamic_index_in_dim(weight_rows, slot, 0, keepdims=False)
        masked_slot = lax.dynamic_index_in_dim(masked, slot, 0, keepdims=False)
        weighted = (left.astype(jnp.float32) * row_weight[:, None]).astype(jnp.bfloat16)
        left_sq = left * left
        cross = jnp.einsum("si,sj->ij", weighted, right, preferred_element_type=jnp.float32)
        moment = jnp.einsum("si,sj->ij", left_sq, masked_slot, preferred_element_type=jnp.float32)
        stacked = jnp.stack([cross, moment], axis=1)[:, :, None, :]
        return lax.dynamic_update_slice_in_dim(buffer, stacked, slot, 2)

    start_buffer = jnp.zeros((rows * lax.axis_size("samp"), 2, width_slots, BLOCK), jnp.float32)
    shares = lax.psum_scatter(
        lax.fori_loop(0, width_slots, one_slot, start_buffer),
        "samp",
        scatter_dimension=0,
        tiled=True,
    )
    zvalue = shares[:, 0] / jnp.sqrt(spread_var * shares[:, 1] + 1e-06)
    row_sums = jnp.sum(zvalue, axis=2)
    col_sums = jnp.sum(zvalue, axis=0)
    live_float = live_slot.astype(jnp.float32)
    first_hot = (first_at[:, None] == block_ids[None, :]).astype(jnp.float32) * live_float[:, None]
    second_hot = (second_at[:, None] == block_ids[None, :]).astype(jnp.float32) * live_float[
        :, None
    ]
    by_column = jnp.dot(second_hot.T, col_sums, precision=highest)
    by_row = jnp.dot(first_hot.T, row_sums.T, precision=highest)
    row_start = lax.axis_index("samp") * rows
    placed = lax.dynamic_update_slice_in_dim(
        jnp.zeros((blocks, BLOCK), jnp.float32), by_row, row_start, 1
    )
    partial_scores = (by_column + placed).reshape(blocks * BLOCK)
    group_part = lax.psum_scatter(partial_scores, "snp", scatter_dimension=0, tiled=True)
    totals = lax.psum(group_part, "samp")
    return totals / math.sqrt(2 * BLOCK)


HALVES = 2
RING = [(0, dz, dx, 0) for dz in range(4) for dx in range(2)][1:]
COLUMN = [(0, 0, 0, 1), (1, 0, 0, 0), (1, 0, 0, 1)]
CHIPS = [(dy, dz, dx, 0) for dy in range(2) for dz in range(4) for dx in range(2)][1:]


def flip(bit, change):
    return 1 - bit if change else bit


def two_groups_kernel(
    list_hbm, slot_hbm, count_hbm, dos_ref, res_ref, out_ref,
    list_ref, slot_ref, count_ref, mine, other, residuals, left_weighted, left_masked, right_weight,
    square_sum, cross, moment, parts, parts_in, vecs, vecs_in, chip, chip_in,
    local_sem, mate_sem, mate_send, far_sem, far_send, res_sem, res_send,
    sum_sem, sum_send, part_sem, part_send, vec_sem, vec_send, chip_sem, chip_send, round_sem,
):
    y = lax.axis_index("snp")
    k = lax.axis_index("samp")
    z, x, c = k // 4, (k // 2) % 2, k % 2
    rows = dos_ref.shape[0]
    own = c + y - 2 * c * y
    share = BLOCK // 8
    width = BLOCK // HALVES
    mesh_id = pl.DeviceIdType.MESH

    def at(dy, dz, dx, dc):
        return (flip(y, dy), ((z + dz) % 4 * 2 + flip(x, dx)) * 2 + flip(c, dc))

    def column(start, size):
        return pl.ds(pl.multiple_of(start, 128), size)

    def remote(src, dst, send, recv, to):
        copy = pltpu.make_async_remote_copy(
            src_ref=src, dst_ref=dst, send_sem=send, recv_sem=recv,
            device_id=to, device_id_type=mesh_id,
        )
        copy.start()
        return copy

    def take(sem, like):
        pltpu.make_async_copy(like, like, sem).wait()

    def greet(sem, *offset):
        pl.semaphore_signal(sem, inc=1, device_id=at(*offset), device_id_type=mesh_id)

    def greet_neighbours(sem):
        greet(sem, 0, 0, 1, 0)

        @pl.when(z > 0)
        def _():
            greet(sem, 0, 3, 0, 0)

        @pl.when(z < 3)
        def _():
            greet(sem, 0, 1, 0, 0)

    neighbours = 1 + jnp.where(z > 0, 1, 0) + jnp.where(z < 3, 1, 0)
    barrier = pltpu.get_barrier_semaphore()
    for offset in COLUMN:
        greet(barrier, *offset)
    greet_neighbours(barrier)
    local = [
        pltpu.make_async_copy(dos_ref.at[:, column(own * BLOCK, BLOCK)], mine.at[0], local_sem.at[0]),
        pltpu.make_async_copy(res_ref, residuals.at[0, 0], local_sem.at[1]),
        pltpu.make_async_copy(list_hbm, list_ref, local_sem.at[2]),
        pltpu.make_async_copy(slot_hbm, slot_ref, local_sem.at[3]),
        pltpu.make_async_copy(count_hbm, count_ref, local_sem.at[4]),
    ]
    for copy in local:
        copy.start()
    pl.semaphore_wait(barrier, len(COLUMN) + neighbours)

    far = []
    for half in range(HALVES):
        for dc in range(2):
            far.append(
                remote(
                    dos_ref.at[:, column(flip(c, dc) * BLOCK + half * width, width)],
                    other.at[half, dc],
                    far_send.at[half, dc], far_sem.at[half, dc], at(1, 0, 0, dc),
                )
            )
    mate_res = remote(res_ref, residuals.at[1, 0], res_send, res_sem, at(0, 0, 0, 1))
    mate_block = remote(
        dos_ref.at[:, column((1 - own) * BLOCK, BLOCK)], mine.at[1], mate_send, mate_sem, at(0, 0, 0, 1)
    )
    greet_neighbours(round_sem.at[0])
    for copy in local:
        copy.wait()

    own_slot, far_slot = 2 * y + own, 2 * (1 - y) + c
    count = jnp.int32(0)
    for pair in range(4):
        first = slot_ref[list_ref[0, pair]]
        second = slot_ref[list_ref[1, pair]]
        here = ((first == own_slot) & (second == far_slot)) | (
            (first == far_slot) & (second == own_slot)
        )
        count = count + jnp.where(here, count_ref[pair], 0)
    hot_group = jnp.where(slot_ref[list_ref[0, 0]] >= 2, 1, 0)
    hot_here = jnp.where(hot_group == y, 1, 0)

    for dc in range(2):
        if dc == 1:
            pl.semaphore_wait(round_sem.at[0], neighbours)
            greet_neighbours(round_sem.at[1])
            mate_res.wait_recv()
            mate_block.wait_recv()
        base = (k - c + flip(c, dc)) * rows
        live = (base + lax.broadcasted_iota(jnp.int32, (1, rows), 1) < count).astype(jnp.float32)
        pick = jnp.full((1, rows), hot_here, jnp.int32) == 1
        weight = residuals[dc]
        left = mine[dc].T.astype(jnp.float32)
        left_weighted[dc] = (left * (jnp.where(pick, weight, 1.0) * live)).astype(jnp.bfloat16)
        left_sq = (left * left).astype(jnp.bfloat16).astype(jnp.float32)
        left_masked[dc] = (left_sq * live).astype(jnp.bfloat16)
        right_weight[dc] = jnp.broadcast_to(jnp.where(pick, 1.0, weight), (width, rows)).T
    pl.semaphore_wait(round_sem.at[1], neighbours)
    greet_neighbours(round_sem.at[2])
    pl.semaphore_wait(round_sem.at[2], neighbours)
    greet(round_sem.at[3], 1, 0, 0, 0)
    both = residuals[0] * residuals[0] + residuals[1] * residuals[1]
    square_sum[0] = jnp.broadcast_to(jnp.sum(both, axis=1, keepdims=True), (8, 128))
    for place, offset in enumerate(RING):
        remote(square_sum.at[0], square_sum.at[place + 1], sum_send, sum_sem, at(*offset))
    pl.semaphore_wait(round_sem.at[3], 1)
    for half in range(HALVES):
        for dc in range(2):
            far[2 * half + dc].wait_recv()
            right = other[half, dc].astype(jnp.float32)
            weighted = (right * right_weight[dc]).astype(jnp.bfloat16)
            squares = (right * right).astype(jnp.bfloat16)
            cross_part = jnp.dot(left_weighted[dc], weighted, preferred_element_type=jnp.float32)
            moment_part = jnp.dot(left_masked[dc], squares, preferred_element_type=jnp.float32)
            if dc == 0:
                cross[half] = cross_part.reshape(8, share, width)
                moment[half] = moment_part.reshape(8, share, width)
            else:
                cross_all = cross[half] + cross_part.reshape(8, share, width)
                moment_all = moment[half] + moment_part.reshape(8, share, width)
                cross[half] = cross_all
                moment[half] = moment_all
                parts[half, :, :share, :] = cross_all.astype(jnp.bfloat16)
                parts[half, :, share:, :] = moment_all.astype(jnp.bfloat16)
        for place, offset in enumerate(RING):
            to = at(*offset)
            remote(
                parts.at[half, to[1] // 2], parts_in.at[half, place],
                part_send.at[half], part_sem.at[half], to,
            )
    others = square_sum.at[pl.ds(1, len(RING))]
    take(sum_sem, others)
    total = square_sum[0]
    for place in range(len(RING)):
        total += square_sum[place + 1]
    spread_var = total[0:1, 0:1] / (rows * 16)
    row_sums = jnp.zeros((share, 1), jnp.float32)
    for half in range(HALVES):
        cross_sum = cross[half, k // 2]
        moment_sum = moment[half, k // 2]
        take(part_sem.at[half], parts_in.at[half])
        for place in range(len(RING)):
            cross_sum += parts_in[half, place, :share, :].astype(jnp.float32)
            moment_sum += parts_in[half, place, share:, :].astype(jnp.float32)
        zvalue = cross_sum / jnp.sqrt(spread_var * moment_sum + 1e-06)
        row_sums += jnp.sum(zvalue, axis=1, keepdims=True)
        vecs[1, :, half * width : (half + 1) * width] = jnp.sum(zvalue, axis=0, keepdims=True)
    row_at = lax.broadcasted_iota(jnp.int32, (share, BLOCK), 0) + share * (k // 2)
    spot = row_at == lax.broadcasted_iota(jnp.int32, (share, BLOCK), 1)
    vecs[0] = jnp.sum(jnp.where(spot, row_sums, 0.0), axis=0, keepdims=True)
    mate_vecs = remote(vecs, vecs_in, vec_send, vec_sem, at(0, 0, 0, 1))
    mate_vecs.wait_recv()
    for group, block_here in ((0, own), (1, c)):
        here, there = vecs[group], vecs_in[group]
        for block in range(2):
            pick = jnp.full((1, BLOCK), block_here, jnp.int32) == block
            chip[group, block : block + 1, :] = jnp.where(pick, here, there)
    for place, offset in enumerate(CHIPS):
        remote(chip.at[offset[0]], chip_in.at[place + 1], chip_send, chip_sem, at(*offset))
    chip_in[0] = chip[0]
    other_chips = chip_in.at[pl.ds(1, len(CHIPS))]
    take(chip_sem, other_chips)
    score = jnp.sum(chip_in[...], axis=0) * (1.0 / math.sqrt(2 * BLOCK))
    for row in range(4):
        lane = row % 2 * 128
        out_ref[row : row + 1, :] = score[row // 2 : row // 2 + 1, lane : lane + 128]
    for copy in far + [mate_res, mate_block, mate_vecs]:
        copy.wait_send()
    take(sum_send, others)
    for half in range(HALVES):
        take(part_send.at[half], parts_in.at[half])
    take(chip_send, other_chips)


def two_groups(dosages, residual, pair_list, block_slot, pair_counts):
    rows = dosages.shape[0]
    width = BLOCK // HALVES
    dma = pltpu.SemaphoreType.DMA
    peers = len(RING)
    hbm = pl.BlockSpec(memory_space=pltpu.HBM)
    half_type, full_type = jnp.bfloat16, jnp.float32
    score = pl.pallas_call(
        two_groups_kernel,
        out_shape=jax.ShapeDtypeStruct((BLOCK // 64, 128), jnp.float32),
        in_specs=[hbm, hbm, hbm, hbm, hbm],
        out_specs=pl.BlockSpec(memory_space=pltpu.VMEM),
        scratch_shapes=[
            pltpu.SMEM((2, 4), jnp.int32),
            pltpu.SMEM((4,), jnp.int32),
            pltpu.SMEM((4,), jnp.int32),
            pltpu.VMEM((2, rows, BLOCK), half_type),
            pltpu.VMEM((HALVES, 2, rows, width), half_type),
            pltpu.VMEM((2, 1, rows), full_type),
            pltpu.VMEM((2, BLOCK, rows), half_type),
            pltpu.VMEM((2, BLOCK, rows), half_type),
            pltpu.VMEM((2, rows, width), full_type),
            pltpu.VMEM((peers + 1, 8, 128), full_type),
            pltpu.VMEM((HALVES, 8, BLOCK // 8, width), full_type),
            pltpu.VMEM((HALVES, 8, BLOCK // 8, width), full_type),
            pltpu.VMEM((HALVES, 8, BLOCK // 4, width), half_type),
            pltpu.VMEM((HALVES, peers, BLOCK // 4, width), half_type),
            pltpu.VMEM((2, 1, BLOCK), full_type),
            pltpu.VMEM((2, 1, BLOCK), full_type),
            pltpu.VMEM((2, 2, BLOCK), full_type),
            pltpu.VMEM((len(CHIPS) + 1, 2, BLOCK), full_type),
            dma((5,)), dma, dma, dma((HALVES, 2)), dma((HALVES, 2)), dma, dma,
            dma, dma, dma((HALVES,)), dma((HALVES,)), dma, dma, dma, dma,
            pltpu.SemaphoreType.REGULAR((4,)),
        ],
        compiler_params=pltpu.CompilerParams(
            collective_id=0, has_side_effects=True, vmem_limit_bytes=62 * 1024 * 1024
        ),
        name="pair_scores",
    )(pair_list.T, block_slot, pair_counts, dosages, residual)
    return score.reshape(2 * BLOCK)


def solution(mesh):
    def on_device(dosages, residual, pair_list, block_slot, pair_counts):
        groups, shards = lax.axis_size("snp"), lax.axis_size("samp")
        fits = groups == 2 and shards == 16 and block_slot.shape[0] == 4
        run = two_groups if fits else any_groups
        return run(dosages, residual, pair_list, block_slot, pair_counts)

    return jax.shard_map(
        on_device,
        mesh=mesh,
        in_specs=(P("samp", "snp"), P("samp"), P(), P(), P()),
        out_specs=P("snp"),
        check_vma=False,
    )
```
